32 devices in a mesh: dp: 4 (over y, x), expert: 8 (over z, core).
Axes of the slice: x: 2, y: 2, z: 4, core: 2. Of those that a mesh axis runs over, the one named last changes fastest.
Arguments:
- hidden_acts: bfloat16 [4, 8, 1024, 768], P('dp', 'expert'), may hold values from -6 to 6
- out_grads: bfloat16 [4, 8, 1024, 2048], P('dp', 'expert'), may hold values from -0.29882812 to 0.29882812
- row_counts: int32 [4, 8], P('dp', 'expert'), may hold values from 128 to 1024, as said below
- plan_now: int32 [4, 8], replicated, may hold values from 0 to 2, as said below
- plan_next: int32 [4, 8], replicated, may hold values from 0 to 2, as said below
- master: float32 [3, 768, 2048], P(None, 'expert', 'dp'), may hold values from -6 to 6
- moment_one: float32 [3, 768, 2048], P(None, 'expert', 'dp'), may hold values from -6 to 6
- moment_two: float32 [3, 768, 2048], P(None, 'expert', 'dp'), may hold values from 0.01 to 0.3
Outputs:
- master_new: float32 [3, 768, 2048], P(None, 'expert', 'dp')
- moment_one_new: float32 [3, 768, 2048], P(None, 'expert', 'dp')
- moment_two_new: float32 [3, 768, 2048], P(None, 'expert', 'dp')
- replica_weights: bfloat16 [4, 8, 768, 2048], P('dp', 'expert')
The draws below stay inside these ranges and needn't reach their ends.
Inputs may be any that keep to these rules, and one draw needn't show every extreme that they name: `plan_now`: every expert is named by 1 to 16 devices, and some expert by exactly 16. `plan_next`: every expert is named by 1 to 16 devices, and some expert by exactly 16. `row_counts`: A multiple of 128; rows from it on are padding. Some device has all 1024 rows live.
All inputs are finite; a program needn't handle non-finite values.
Results may differ from the reference program's by a relative error of at most 0.005.
Values may be sent and summed in bfloat16 or wider, within the bound.
No kernel may reach another device: no remote copies, remote signals or barrier semaphores. Data moves between devices by JAX's collectives and lax.ppermute only.
A program may use at most 192 MiB of HBM per device.

```python
import math
import jax
import jax.numpy as jnp
from jax import lax

FF = 768
DW = 2048
ROWS = 1024
MAXREP = 16
GROUPS = 4
OWNERS = 8
SLOTS = 32
EXPERTS = 3


def replica_plan(seed_key):
    count_keys = jax.random.split(jax.random.fold_in(seed_key, 11), EXPERTS)

    def choose(remain, item):
        position, subkey = item
        later = EXPERTS - 1 - position
        lowest = jnp.maximum(1, remain - MAXREP * later)
        highest = jnp.minimum(MAXREP, remain - later)
        drawn = jax.random.randint(subkey, (), lowest, highest + 1, dtype=jnp.int32)
        taken = jnp.where(position == 0, MAXREP, drawn).astype(jnp.int32)
        return (remain - taken, taken)
    unused, counts = lax.scan(choose, jnp.int32(SLOTS), (jnp.arange(EXPERTS, dtype=jnp.int32), count_keys))
    order = jax.random.permutation(jax.random.fold_in(seed_key, 12), EXPERTS)
    counts = counts[order]
    bounds = jnp.cumsum(counts)
    positions = jnp.arange(SLOTS, dtype=jnp.int32)
    owner = jnp.sum((positions[:, None] >= bounds[None, :]).astype(jnp.int32), axis=1)
    owner = jax.random.permutation(jax.random.fold_in(seed_key, 13), owner)
    return owner.reshape(GROUPS, OWNERS).astype(jnp.int32)


def draw_plan_now(key, part):
    return replica_plan(jax.random.fold_in(key, 7))


def draw_plan_next(key, part):
    return replica_plan(jax.random.fold_in(key, 101))


def draw_row_counts(key, part):
    blocks = jax.random.randint(jax.random.fold_in(key, 21), (SLOTS,), 1, ROWS // 128 + 1, dtype=jnp.int32)
    chosen = jax.random.randint(jax.random.fold_in(key, 22), (), 0, SLOTS, dtype=jnp.int32)
    blocks = jnp.where(jnp.arange(SLOTS, dtype=jnp.int32) == chosen, ROWS // 128, blocks)
    return (blocks * 128).reshape(GROUPS, OWNERS).astype(jnp.int32)


def shard_levels(key, shape, cuts, low, top_value):
    loudness, own = 1.0, jax.random.fold_in(key, 6)
    for axis_at, parts in cuts:
        steps = jnp.exp(jax.random.uniform(jax.random.fold_in(own, axis_at), (parts,), jnp.float32, low / len(cuts), top_value / len(cuts)))
        loudness = loudness * jnp.repeat(steps, shape[axis_at] // parts).reshape([-1 if axis == axis_at else 1 for axis in range(len(shape))])
    return loudness


def bell_draw(stream_key, extent, spread, most, pieces=(), kind=jnp.bfloat16):
    values = jax.random.normal(stream_key, extent, jnp.float32) * spread
    if len(pieces) > 0:
        values = shard_levels(stream_key, extent, pieces, -0.22, 0.18) * values
    return jnp.clip(values, min=-most, max=most).astype(kind)


def setup_inputs(seed: int = 0) -> dict:
    key_of = jax.random.split(jax.random.key(seed), 9)
    return {
        "hidden_acts": bell_draw(key_of[0], (GROUPS, OWNERS, ROWS, FF), 1.0, 6.0, ((0, 4), (1, 8))),
        "out_grads": bell_draw(key_of[1], (GROUPS, OWNERS, ROWS, DW), 0.05, 0.29882812, ((0, 4), (1, 8))),
        "row_counts": draw_row_counts(jax.random.fold_in(key_of[8], 71), 0),
        "plan_now": draw_plan_now(jax.random.fold_in(key_of[8], 71), 0),
        "plan_next": draw_plan_next(jax.random.fold_in(key_of[8], 71), 0),
        "master": bell_draw(key_of[5], (EXPERTS, FF, DW), 1.0, 6.0, ((1, 8), (2, 4)), jnp.float32),
        "moment_one": bell_draw(key_of[6], (EXPERTS, FF, DW), 1.0, 6.0, ((1, 8), (2, 4)), jnp.float32),
        "moment_two": jnp.clip(jnp.exp(math.log(0.3) - 3.4011974 * jax.random.uniform(key_of[7], (EXPERTS, FF, DW), jnp.float32) ** shard_levels(key_of[7], (EXPERTS, FF, DW), ((1, 8), (2, 4)), -0.2, 0.2)), 0.01, 0.3),
    }


beta_one = 0.9
beta_two = 0.999
learn_rate = 0.1
epsilon = 1e-08
first_fix = 1.0 - beta_one ** 10
second_fix = 1.0 - beta_two ** 10

def reference(hidden_acts, out_grads, row_counts, plan_now, plan_next, master, moment_one, moment_two):
    row_index = jnp.arange(ROWS, dtype=jnp.int32)
    inputs = (hidden_acts.reshape(SLOTS, ROWS, FF), out_grads.reshape(SLOTS, ROWS, DW), row_counts.reshape(SLOTS), plan_now.reshape(SLOTS))

    def accumulate(running, item):
        hidden, upstream, count, expert = item
        row_mask = (row_index < count).astype(hidden.dtype)[:, None]
        partial_value = lax.dot_general(hidden * row_mask, upstream, (((0,), (0,)), ((), ())), preferred_element_type=jnp.float32).astype(jnp.bfloat16)
        partial_value = lax.optimization_barrier(partial_value)
        current = lax.dynamic_index_in_dim(running, expert, 0, keepdims=False)
        running = lax.dynamic_update_index_in_dim(running, current + partial_value.astype(jnp.float32), expert, 0)
        return (running, None)
    grad_sum, unused = lax.scan(accumulate, jnp.zeros((EXPERTS, FF, DW), jnp.float32), inputs)
    moment_one_new = beta_one * moment_one + (1.0 - beta_one) * grad_sum
    moment_two_new = beta_two * moment_two + (1.0 - beta_two) * grad_sum * grad_sum
    master_new = master - learn_rate * (moment_one_new / first_fix) / (jnp.sqrt(moment_two_new / second_fix) + epsilon)
    rounded = master_new.astype(jnp.bfloat16)
    replica_weights = jnp.take(rounded, plan_next, axis=0)
    return (master_new, moment_one_new, moment_two_new, replica_weights)
```

```python
import functools

import jax
import jax.numpy as jnp
from jax import lax
from jax.experimental import pallas as pl
from jax.experimental.pallas import tpu as pltpu
from jax.sharding import PartitionSpec as P

beta_one = 0.9
beta_two = 0.999
learn_rate = 0.1
epsilon = 1e-08
first_fix = 1.0 - beta_one**10
second_fix = 1.0 - beta_two**10

AXES = ("dp", "expert")


def adam(grad_sum, master, moment_one, moment_two):
    moment_one_new = beta_one * moment_one + (1.0 - beta_one) * grad_sum
    moment_two_new = beta_two * moment_two + (1.0 - beta_two) * grad_sum * grad_sum
    master_new = master - learn_rate * (moment_one_new / first_fix) / (
        jnp.sqrt(moment_two_new / second_fix) + epsilon
    )
    return master_new, moment_one_new, moment_two_new


def matmul_kernel(place, hidden_ref, upstream_ref, keep_ref, send_ref, turned):
    planes, unused, rows, unused = keep_ref.shape

    @pl.when(pl.program_id(0) == 0)
    def turn():
        hidden = hidden_ref[...]
        live = lax.broadcasted_iota(jnp.int32, hidden.shape, 0) < place[3]
        turned[...] = jnp.where(live, hidden, jnp.zeros_like(hidden)).T

    product = jnp.dot(turned[...], upstream_ref[...], preferred_element_type=jnp.float32)
    product = product.astype(jnp.bfloat16)
    even_core = place[2] == 0
    for plane in range(planes):
        even = product[2 * plane * rows : (2 * plane + 1) * rows]
        odd = product[(2 * plane + 1) * rows : (2 * plane + 2) * rows]
        ahead = lax.rem(plane - place[1] + planes, planes)
        keep_ref[ahead, 0] = jnp.where(even_core, even, odd)
        send_ref[ahead, 0] = jnp.where(even_core, odd, even)


def partial_blocks(place, hidden, upstream, groups, planes):
    tokens, inner = hidden.shape
    width = upstream.shape[1]
    cols = width // groups
    rows = inner // (2 * planes)
    out = jax.ShapeDtypeStruct((planes, groups, rows, cols), jnp.bfloat16)
    out_spec = pl.BlockSpec((planes, 1, rows, cols), lambda j, place: (0, j, 0, 0))
    return pl.pallas_call(
        matmul_kernel,
        grid_spec=pltpu.PrefetchScalarGridSpec(
            num_scalar_prefetch=1,
            grid=(groups,),
            in_specs=[
                pl.BlockSpec((tokens, inner), lambda j, place: (0, 0)),
                pl.BlockSpec((tokens, cols), lambda j, place: (0, place[0] ^ j)),
            ],
            out_specs=[out_spec, out_spec],
            scratch_shapes=[pltpu.VMEM((inner, tokens), jnp.bfloat16)],
        ),
        out_shape=[out, out],
        compiler_params=pltpu.CompilerParams(vmem_limit_bytes=40 * 2**20),
        cost_estimate=pl.CostEstimate(
            flops=2 * tokens * inner * width,
            bytes_accessed=2 * (tokens * inner + tokens * width + inner * width),
            transcendentals=0,
        ),
        name="partial_blocks",
    )(place, hidden, upstream)


def assemble_kernel(groups, planes, place, *refs):
    mine = refs[: planes * groups]
    other = refs[planes * groups : planes * groups + planes]
    out_ref = refs[-2]
    sems = refs[-1]
    rows, cols = mine[0].shape[1:]
    copies = []
    for s in range(planes):
        plane = lax.rem(place[1] - s + planes, planes)
        for i in range(2):
            row = pl.multiple_of((2 * plane + (place[2] ^ i)) * rows, rows)
            for j in range(groups):
                col = pl.multiple_of((place[0] ^ j) * cols, cols)
                src = mine[s * groups + j].at[0] if i == 0 else other[s].at[j]
                copies.append(
                    pltpu.make_async_copy(
                        src, out_ref.at[pl.ds(row, rows), pl.ds(col, cols)], sems.at[len(copies)]
                    )
                )
    for copy in copies:
        copy.start()
    for copy in copies:
        copy.wait()


def assemble(place, mine, other, groups, planes):
    rows, cols = mine[0].shape[1:]
    return pl.pallas_call(
        functools.partial(assemble_kernel, groups, planes),
        in_specs=[pl.BlockSpec(memory_space=pltpu.SMEM)]
        + [pl.BlockSpec(memory_space=pl.ANY)] * (len(mine) + len(other)),
        out_specs=pl.BlockSpec(memory_space=pl.ANY),
        scratch_shapes=[pltpu.SemaphoreType.DMA((2 * planes * groups,))],
        out_shape=jax.ShapeDtypeStruct((2 * planes * rows, groups * cols), jnp.bfloat16),
        cost_estimate=pl.CostEstimate(
            flops=0, bytes_accessed=8 * planes * rows * groups * cols, transcendentals=0
        ),
        name="assemble",
    )(place, *mine, *other)


def per_device_planes(
    hidden_acts, out_grads, row_counts, plan_now, plan_next, master, moment_one, moment_two
):
    groups = lax.axis_size("dp")
    owners = lax.axis_size("expert")
    planes = owners // 2
    group = lax.axis_index("dp")
    owner = lax.axis_index("expert")
    plane, core = owner // 2, owner % 2
    experts = master.shape[0]
    place = jnp.stack([group, plane, core, row_counts[0, 0]]).astype(jnp.int32)

    everyone = range(groups * owners)
    to_core = [(d, d ^ 1) for d in everyone]
    to_group = [[(d, d ^ (j * owners)) for d in everyone] for j in range(groups)]
    to_plane = [
        [(d, d // owners * owners + (d % owners + 2 * s) % owners) for d in everyone] for s in range(planes)
    ]
    order = sorted(range(planes), key=lambda s: -min(s, planes - s))

    near_groups = jnp.stack([group ^ j for j in range(groups)])
    near_owners = jnp.stack([owner, owner ^ 1])
    now = plan_now[near_groups][:, near_owners]
    later = plan_next[near_groups][:, near_owners]

    keep, send = partial_blocks(place, hidden_acts[0, 0], out_grads[0, 0], groups, planes)
    held = lax.ppermute(send, AXES, to_core)

    arrived = {}
    own_sum = None
    for s in order:
        sums = [jnp.float32(0.0)] * experts
        for j in range(groups):
            block = jnp.stack([keep[s, j], held[s, j]])
            if j:
                block = lax.ppermute(block, AXES, to_group[j])
            block = block.astype(jnp.float32)
            for i in range(2):
                sums = [
                    sums[e] + jnp.where(now[j, i] == e, block[i], jnp.float32(0.0)) for e in range(experts)
                ]
        total = jnp.stack(sums)
        if s:
            arrived[s] = lax.ppermute(total.astype(jnp.bfloat16), AXES, to_plane[s])
        else:
            own_sum = total
    grad_sum = own_sum
    for s in range(1, planes):
        grad_sum = grad_sum + arrived[s].astype(jnp.float32)

    master_new, moment_one_new, moment_two_new = adam(grad_sum, master, moment_one, moment_two)
    rounded = master_new.astype(jnp.bfloat16)

    mine = {}
    other = {}
    for s in order[::-1]:
        shard = lax.ppermute(rounded, AXES, to_plane[s]) if s else rounded
        passed_on = []
        for j in range(groups):
            block = jnp.stack(
                [lax.dynamic_index_in_dim(shard, later[j, i], 0, keepdims=False) for i in range(2)]
            )
            if j:
                block = lax.ppermute(block, AXES, to_group[j])
            mine[s, j] = block
            passed_on.append(block[1])
        other[s] = lax.ppermute(jnp.stack(passed_on), AXES, to_core)
    replica = assemble(
        place,
        [mine[s, j] for s in range(planes) for j in range(groups)],
        [other[s] for s in range(planes)],
        groups,
        planes,
    )
    return (master_new, moment_one_new, moment_two_new, replica[None, None])


def per_device_whole(
    hidden_acts, out_grads, row_counts, plan_now, plan_next, master, moment_one, moment_two
):
    ex_count = lax.axis_size("expert")
    dp_index = lax.axis_index("dp")
    experts = master.shape[0]
    piece_rows = master.shape[1]
    hidden = hidden_acts[0, 0]
    upstream = out_grads[0, 0]
    width = upstream.shape[1]
    row_index = jnp.arange(hidden.shape[0], dtype=jnp.int32)
    row_mask = (row_index < row_counts[0, 0]).astype(hidden.dtype)[:, None]
    partial_value = lax.dot_general(
        hidden * row_mask, upstream, (((0,), (0,)), ((), ())), preferred_element_type=jnp.float32
    ).astype(jnp.bfloat16)
    expert_ids = jnp.arange(experts, dtype=jnp.int32)
    pieces = lax.all_to_all(
        partial_value.reshape(ex_count, piece_rows, width),
        "expert",
        split_axis=0,
        concat_axis=0,
        tiled=True,
    )
    sender_ids = lax.dynamic_index_in_dim(plan_now, dp_index, 0, keepdims=False)
    onehot = (sender_ids[None, :] == expert_ids[:, None]).astype(jnp.bfloat16)
    totals = jnp.einsum("es,srd->erd", onehot, pieces, preferred_element_type=jnp.float32)
    grad_sum = lax.psum_scatter(
        totals.astype(jnp.bfloat16), "dp", scatter_dimension=2, tiled=True
    ).astype(jnp.float32)
    master_new, moment_one_new, moment_two_new = adam(grad_sum, master, moment_one, moment_two)
    rounded = master_new.astype(jnp.bfloat16)
    full_cols = lax.all_gather(rounded, "dp", axis=2, tiled=True)
    targets = lax.dynamic_index_in_dim(plan_next, dp_index, 0, keepdims=False)
    outgoing = jnp.take(full_cols, targets, axis=0)
    incoming = lax.all_to_all(outgoing, "expert", split_axis=0, concat_axis=0, tiled=True)
    replica = incoming.reshape(ex_count * piece_rows, width)
    return (master_new, moment_one_new, moment_two_new, replica[None, None])


def per_device(hidden_acts, out_grads, row_counts, plan_now, plan_next, master, *moments):
    groups = lax.axis_size("dp")
    owners = lax.axis_size("expert")
    experts, rows, cols = master.shape
    few = experts <= 2 * groups and owners <= 8
    even = owners % 2 == 0 and groups & (groups - 1) == 0 and rows % 16 == 0 and cols % 128 == 0
    body = per_device_planes if few and even else per_device_whole
    return body(hidden_acts, out_grads, row_counts, plan_now, plan_next, master, *moments)


def solution(mesh):
    return jax.shard_map(
        per_device,
        mesh=mesh,
        in_specs=(
            P("dp", "expert", None, None),
            P("dp", "expert", None, None),
            P("dp", "expert"),
            P(),
            P(),
            P(None, "expert", "dp"),
            P(None, "expert", "dp"),
            P(None, "expert", "dp"),
        ),
        out_specs=(
            P(None, "expert", "dp"),
            P(None, "expert", "dp"),
            P(None, "expert", "dp"),
            P("dp", "expert", None, None),
        ),
        check_vma=False,
    )
```

```python
import jax
import jax.numpy as jnp
from jax import lax
from jax.experimental import pallas as pl
from jax.experimental.pallas import tpu as pltpu
from jax.sharding import PartitionSpec as P

beta_one = 0.9
beta_two = 0.999
learn_rate = 0.1
epsilon = 1e-08
first_fix = 1.0 - beta_one**10
second_fix = 1.0 - beta_two**10

AXES = ("dp", "expert")


def adam(grad_sum, master, moment_one, moment_two):
    moment_one_new = beta_one * moment_one + (1.0 - beta_one) * grad_sum
    moment_two_new = beta_two * moment_two + (1.0 - beta_two) * grad_sum * grad_sum
    master_new = master - learn_rate * (moment_one_new / first_fix) / (
        jnp.sqrt(moment_two_new / second_fix) + epsilon
    )
    return master_new, moment_one_new, moment_two_new


def matmul_kernel(place, now_ref, next_ref, hidden_ref, upstream_ref, keep_ref, send_ref, chosen_ref, turned):
    planes, unused, rows, unused = keep_ref.shape
    experts = chosen_ref.shape[2]

    @pl.when(pl.program_id(0) == 0)
    def turn():
        hidden = hidden_ref[...]
        live = lax.broadcasted_iota(jnp.int32, hidden.shape, 0) < place[3]
        turned[...] = jnp.where(live, hidden, jnp.zeros_like(hidden)).T
        shape = chosen_ref.shape[2:]
        names = lax.broadcasted_iota(jnp.int32, shape, 0)
        for n, plan_ref in enumerate((now_ref, next_ref)):
            for near in range(chosen_ref.shape[1]):
                named = plan_ref[place[0] ^ (near // 2), 2 * place[1] + (place[2] ^ (near % 2))]
                chosen_ref[n, near] = jnp.where(names == named, 1.0, 0.0)

    product = jnp.dot(turned[...], upstream_ref[...], preferred_element_type=jnp.float32)
    product = product.astype(jnp.bfloat16)
    even_core = place[2] == 0
    for plane in range(planes):
        even = product[2 * plane * rows : (2 * plane + 1) * rows]
        odd = product[(2 * plane + 1) * rows : (2 * plane + 2) * rows]
        ahead = lax.rem(plane - place[1] + planes, planes)
        keep_ref[ahead, 0] = jnp.where(even_core, even, odd)
        send_ref[ahead, 0] = jnp.where(even_core, odd, even)


def partial_blocks(place, plan_now, plan_next, hidden, upstream, experts):
    groups, owners = plan_now.shape
    planes = owners // 2
    tokens, inner = hidden.shape
    width = upstream.shape[1]
    cols = width // groups
    rows = inner // owners
    out = jax.ShapeDtypeStruct((planes, groups, rows, cols), jnp.bfloat16)
    chosen = jax.ShapeDtypeStruct((2, 2 * groups, experts, cols), jnp.float32)
    out_spec = pl.BlockSpec((planes, 1, rows, cols), lambda j, place: (0, j, 0, 0))
    smem = pl.BlockSpec(memory_space=pltpu.SMEM)
    return pl.pallas_call(
        matmul_kernel,
        grid_spec=pltpu.PrefetchScalarGridSpec(
            num_scalar_prefetch=1,
            grid=(groups,),
            in_specs=[
                smem,
                smem,
                pl.BlockSpec((tokens, inner), lambda j, place: (0, 0)),
                pl.BlockSpec((tokens, cols), lambda j, place: (0, place[0] ^ j)),
            ],
            out_specs=[out_spec, out_spec, pl.BlockSpec(chosen.shape, lambda j, place: (0, 0, 0, 0))],
            scratch_shapes=[pltpu.VMEM((inner, tokens), jnp.bfloat16)],
        ),
        out_shape=[out, out, chosen],
        compiler_params=pltpu.CompilerParams(vmem_limit_bytes=60 * 2**20),
        cost_estimate=pl.CostEstimate(
            flops=2 * tokens * inner * width,
            bytes_accessed=2 * (tokens * inner + tokens * width + inner * width),
            transcendentals=0,
        ),
        name="partial_blocks",
    )(place, plan_now, plan_next, hidden, upstream)


def after(values, token):
    if token is None:
        return values
    return list(lax.optimization_barrier((*values, token))[:-1])


def per_device_planes(
    hidden_acts, out_grads, row_counts, plan_now, plan_next, master, moment_one, moment_two
):
    groups = lax.axis_size("dp")
    owners = lax.axis_size("expert")
    planes = owners // 2
    group = lax.axis_index("dp")
    owner = lax.axis_index("expert")
    plane, core = owner // 2, owner % 2
    experts, rows, cols = master.shape
    place = jnp.stack([group, plane, core, row_counts[0, 0]]).astype(jnp.int32)

    everyone = range(groups * owners)
    to_core = [(d, d ^ 1) for d in everyone]
    to_group = [[(d, d ^ (j * owners)) for d in everyone] for j in range(groups)]
    to_plane = [
        [(d, d // owners * owners + (d % owners + 2 * s) % owners) for d in everyone] for s in range(planes)
    ]
    order = sorted(range(planes), key=lambda s: -min(s, planes - s))

    keep, send, chosen = partial_blocks(
        place, plan_now, plan_next, hidden_acts[0, 0], out_grads[0, 0], experts
    )
    now, later = chosen[0], chosen[1]
    held = lax.ppermute(send, AXES, to_core)

    sums = []
    arrived = []
    for n, s in enumerate(order):
        messages = [jnp.stack([keep[s, j], held[s, j]]) for j in range(groups)]
        messages = after(messages, sums[n - 2] if n >= 2 else None)
        total = jnp.zeros((experts, rows, cols), jnp.float32)
        for j in range(groups):
            block = lax.ppermute(messages[j], AXES, to_group[j]) if j else messages[j]
            for i in range(2):
                total = total + now[2 * j + i][:, None] * block[i].astype(jnp.float32)
        if s:
            sums.append(total.astype(jnp.bfloat16))
            arrived.append(lax.ppermute(sums[-1], AXES, to_plane[s]))
    grad_sum = total
    for shard in arrived:
        grad_sum = grad_sum + shard.astype(jnp.float32)

    master_new, moment_one_new, moment_two_new = adam(grad_sum, master, moment_one, moment_two)
    rounded = master_new.astype(jnp.bfloat16)

    def in_order(blocks):
        for bit in range(groups.bit_length() - 1):
            swap = (group >> bit) % 2 == 1
            blocks = [jnp.where(swap, blocks[m ^ (1 << bit)], blocks[m]) for m in range(groups)]
        return jnp.concatenate(blocks, axis=-1)

    replica = jnp.zeros((planes, 2, rows, groups * cols), jnp.bfloat16)
    for s in order[::-1]:
        shard = (lax.ppermute(rounded, AXES, to_plane[s]) if s else rounded).astype(jnp.float32)
        blocks = []
        for j in range(groups):
            block = jnp.stack(
                [jnp.sum(later[2 * j + i][:, None] * shard, axis=0).astype(jnp.bfloat16) for i in range(2)]
            )
            blocks.append(lax.ppermute(block, AXES, to_group[j]) if j else block)
        mine = in_order([block[0] for block in blocks])
        other = lax.ppermute(jnp.stack([block[1] for block in blocks]), AXES, to_core)
        other = in_order([other[j] for j in range(groups)])
        both = jnp.stack([jnp.where(core == 0, mine, other), jnp.where(core == 0, other, mine)])
        replica = lax.dynamic_update_index_in_dim(replica, both, (plane - s) % planes, 0)
    replica = replica.reshape(2 * planes * rows, groups * cols)
    return (master_new, moment_one_new, moment_two_new, replica[None, None])


def per_device_whole(
    hidden_acts, out_grads, row_counts, plan_now, plan_next, master, moment_one, moment_two
):
    ex_count = lax.axis_size("expert")
    dp_index = lax.axis_index("dp")
    experts = master.shape[0]
    piece_rows = master.shape[1]
    hidden = hidden_acts[0, 0]
    upstream = out_grads[0, 0]
    width = upstream.shape[1]
    row_index = jnp.arange(hidden.shape[0], dtype=jnp.int32)
    row_mask = (row_index < row_counts[0, 0]).astype(hidden.dtype)[:, None]
    partial_value = lax.dot_general(
        hidden * row_mask, upstream, (((0,), (0,)), ((), ())), preferred_element_type=jnp.float32
    ).astype(jnp.bfloat16)
    expert_ids = jnp.arange(experts, dtype=jnp.int32)
    pieces = lax.all_to_all(
        partial_value.reshape(ex_count, piece_rows, width),
        "expert",
        split_axis=0,
        concat_axis=0,
        tiled=True,
    )
    sender_ids = lax.dynamic_index_in_dim(plan_now, dp_index, 0, keepdims=False)
    onehot = (sender_ids[None, :] == expert_ids[:, None]).astype(jnp.bfloat16)
    totals = jnp.einsum("es,srd->erd", onehot, pieces, preferred_element_type=jnp.float32)
    grad_sum = lax.psum_scatter(
        totals.astype(jnp.bfloat16), "dp", scatter_dimension=2, tiled=True
    ).astype(jnp.float32)
    master_new, moment_one_new, moment_two_new = adam(grad_sum, master, moment_one, moment_two)
    rounded = master_new.astype(jnp.bfloat16)
    full_cols = lax.all_gather(rounded, "dp", axis=2, tiled=True)
    targets = lax.dynamic_index_in_dim(plan_next, dp_index, 0, keepdims=False)
    outgoing = jnp.take(full_cols, targets, axis=0)
    incoming = lax.all_to_all(outgoing, "expert", split_axis=0, concat_axis=0, tiled=True)
    replica = incoming.reshape(ex_count * piece_rows, width)
    return (master_new, moment_one_new, moment_two_new, replica[None, None])


def per_device(hidden_acts, out_grads, row_counts, plan_now, plan_next, master, *moments):
    groups = lax.axis_size("dp")
    owners = lax.axis_size("expert")
    experts, rows, cols = master.shape
    few = experts <= 2 * groups and owners <= 8
    even = owners % 2 == 0 and groups & (groups - 1) == 0 and rows % 16 == 0 and cols % 128 == 0
    body = per_device_planes if few and even else per_device_whole
    return body(hidden_acts, out_grads, row_counts, plan_now, plan_next, master, *moments)


def solution(mesh):
    return jax.shard_map(
        per_device,
        mesh=mesh,
        in_specs=(
            P("dp", "expert", None, None),
            P("dp", "expert", None, None),
            P("dp", "expert"),
            P(),
            P(),
            P(None, "expert", "dp"),
            P(None, "expert", "dp"),
            P(None, "expert", "dp"),
        ),
        out_specs=(
            P(None, "expert", "dp"),
            P(None, "expert", "dp"),
            P(None, "expert", "dp"),
            P("dp", "expert", None, None),
        ),
        check_vma=False,
    )
```

```python
import jax
import jax.numpy as jnp
from jax import lax
from jax.experimental import pallas as pl
from jax.experimental.pallas import tpu as pltpu
from jax.sharding import PartitionSpec as P

beta_one = 0.9
beta_two = 0.999
learn_rate = 0.1
epsilon = 1e-08
first_fix = 1.0 - beta_one**10
second_fix = 1.0 - beta_two**10

AXES = ("dp", "expert")


def adam(grad_sum, master, moment_one, moment_two):
    moment_one_new = beta_one * moment_one + (1.0 - beta_one) * grad_sum
    moment_two_new = beta_two * moment_two + (1.0 - beta_two) * grad_sum * grad_sum
    master_new = master - learn_rate * (moment_one_new / first_fix) / (
        jnp.sqrt(moment_two_new / second_fix) + epsilon
    )
    return master_new, moment_one_new, moment_two_new


def plane_order(planes):
    return sorted(range(planes), key=lambda s: -min(s, planes - s))


def store_blocks(product, even_core, rows, at, j, keep_ref, send_ref):
    even, odd = product[:rows], product[rows:]
    keep_ref[at, j] = jnp.where(even_core, even, odd).astype(keep_ref.dtype)
    send_ref[at, j] = jnp.where(even_core, odd, even).astype(send_ref.dtype)


def first_kernel(
    count_ref, now_hbm, next_hbm, hidden_hbm, upstream_hbm, turned_ref, upstream_ref, keep_ref, send_ref,
    chosen_ref, hidden_ref, now_ref, next_ref, sems, small_sems,
):
    tokens, inner = hidden_ref.shape
    groups, rows, cols = keep_ref.shape[1:]
    planes = inner // (2 * rows)
    parts = sems.shape[1]
    part = tokens // parts
    group, owner = lax.axis_index("dp"), lax.axis_index("expert")
    plane, core = owner >> 1, owner & 1

    smalls = [
        pltpu.make_async_copy(source, target, small_sems.at[n])
        for n, (source, target) in enumerate(((now_hbm, now_ref), (next_hbm, next_ref)))
    ]
    for copy in smalls:
        copy.start()
    copies = []
    for n in range(parts):
        at = pl.ds(n * part, part)
        copies.append(
            [
                pltpu.make_async_copy(hidden_hbm.at[at], hidden_ref.at[at], sems.at[0, n]),
                pltpu.make_async_copy(upstream_hbm.at[at], upstream_ref.at[at], sems.at[1, n]),
            ]
        )
    for kind in range(2):
        for copy in copies:
            copy[kind].start()

    for copy in smalls:
        copy.wait()
    names = lax.broadcasted_iota(jnp.int32, chosen_ref.shape[2:], 0)
    for n, plan_ref in enumerate((now_ref, next_ref)):
        for near in range(2 * groups):
            named = plan_ref[group ^ (near // 2), 2 * plane + (core ^ (near % 2))]
            chosen_ref[n, near] = jnp.where(names == named, 1.0, 0.0)

    for n in range(parts):
        copies[n][0].wait()
        hidden = hidden_ref[n * part : (n + 1) * part]
        live = lax.broadcasted_iota(jnp.int32, hidden.shape, 0) < count_ref[0, 0] - n * part
        hidden = jnp.where(live, hidden, jnp.zeros_like(hidden)).T
        for m, s in enumerate(plane_order(planes)):
            for p in range(planes):

                @pl.when(lax.rem(plane + s, planes) == p)
                def put():
                    turned_ref[2 * rows * m : 2 * rows * (m + 1), n * part : (n + 1) * part] = hidden[
                        2 * rows * p : 2 * rows * (p + 1)
                    ]
    for n in range(parts):
        copies[n][1].wait()

    def columns(j, carry):
        at = pl.ds(pl.multiple_of((group ^ j) * cols, cols), cols)
        product = jnp.dot(
            turned_ref[: 2 * rows], upstream_ref[:, at], preferred_element_type=jnp.float32
        )
        store_blocks(product, core == 0, rows, 0, j, keep_ref, send_ref)
        return carry

    lax.fori_loop(0, groups, columns, 0)


def rest_kernel(turned_ref, upstream_ref, keep_ref, send_ref):
    rest, groups, rows, cols = keep_ref.shape
    group, core = lax.axis_index("dp"), lax.axis_index("expert") & 1

    def columns(j, carry):
        at = pl.ds(pl.multiple_of((group ^ j) * cols, cols), cols)
        product = jnp.dot(
            turned_ref[2 * rows :], upstream_ref[:, at], preferred_element_type=jnp.float32
        )
        for n in range(rest):
            part = product[2 * rows * n : 2 * rows * (n + 1)]
            store_blocks(part, core == 0, rows, n, j, keep_ref, send_ref)
        return carry

    lax.fori_loop(0, groups, columns, 0)


def first_blocks(counts, plan_now, plan_next, hidden, upstream, experts):
    groups, owners = plan_now.shape
    planes = owners // 2
    plan_now, plan_next, hidden, upstream = [
        pltpu.with_memory_space_constraint(array, pltpu.HBM)
        for array in (plan_now, plan_next, hidden, upstream)
    ]
    tokens, inner = hidden.shape
    width = upstream.shape[1]
    cols = width // groups
    rows = inner // owners
    parts = 4 if tokens % 512 == 0 else 1
    hbm = pl.BlockSpec(memory_space=pltpu.HBM)
    vmem = pl.BlockSpec(memory_space=pltpu.VMEM)

    def blocks(n):
        return jax.ShapeDtypeStruct((n, groups, rows, cols), jnp.bfloat16)

    turned, copied, keep, send, chosen = pl.pallas_call(
        first_kernel,
        in_specs=[pl.BlockSpec(memory_space=pltpu.SMEM)] + [hbm] * 4,
        out_specs=[vmem] * 5,
        out_shape=[
            jax.ShapeDtypeStruct((inner, tokens), jnp.bfloat16),
            jax.ShapeDtypeStruct((tokens, width), jnp.bfloat16),
            blocks(1),
            blocks(1),
            jax.ShapeDtypeStruct((2, 2 * groups, experts, cols), jnp.float32),
        ],
        scratch_shapes=[
            pltpu.VMEM((tokens, inner), jnp.bfloat16),
            pltpu.SMEM(plan_now.shape, jnp.int32),
            pltpu.SMEM(plan_next.shape, jnp.int32),
            pltpu.SemaphoreType.DMA((2, parts)),
            pltpu.SemaphoreType.DMA((2,)),
        ],
        compiler_params=pltpu.CompilerParams(vmem_limit_bytes=24 * 2**20),
        cost_estimate=pl.CostEstimate(
            flops=4 * tokens * rows * width,
            bytes_accessed=2 * (tokens * inner + tokens * width),
            transcendentals=0,
        ),
        name="first_blocks",
    )(counts, plan_now, plan_next, hidden, upstream)
    return turned, copied, keep, send, chosen


def rest_blocks(turned, upstream, groups, planes):
    tokens, width = upstream.shape
    inner = turned.shape[0]
    cols = width // groups
    rows = inner // (2 * planes)
    vmem = pl.BlockSpec(memory_space=pltpu.VMEM)
    out = jax.ShapeDtypeStruct((planes - 1, groups, rows, cols), jnp.bfloat16)
    return pl.pallas_call(
        rest_kernel,
        in_specs=[vmem, vmem],
        out_specs=[vmem, vmem],
        out_shape=[out, out],
        compiler_params=pltpu.CompilerParams(vmem_limit_bytes=24 * 2**20),
        cost_estimate=pl.CostEstimate(
            flops=2 * tokens * (inner - 2 * rows) * width,
            bytes_accessed=2 * (inner - 2 * rows) * width,
            transcendentals=0,
        ),
        name="rest_blocks",
    )(turned, upstream)


class Mail:
    def __init__(self):
        self.arrived = {}

    def send(self, name, value, pairs, after=()):
        self.arrived[name] = lax.ppermute(self.hold(value, after), AXES, pairs)

    def hold(self, value, after):
        if after:
            value, *there = lax.optimization_barrier((value, *[self.arrived[n] for n in after]))
            self.arrived.update(zip(after, there))
        return value

    def __getitem__(self, name):
        return self.arrived[name]


def per_device_planes(
    hidden_acts, out_grads, row_counts, plan_now, plan_next, master, moment_one, moment_two
):
    groups = lax.axis_size("dp")
    owners = lax.axis_size("expert")
    planes = owners // 2
    group = lax.axis_index("dp")
    owner = lax.axis_index("expert")
    plane, core = owner >> 1, owner & 1
    experts, rows, cols = master.shape

    everyone = range(groups * owners)
    to_core = [(d, d ^ 1) for d in everyone]
    to_group = [[(d, d ^ (j * owners)) for d in everyone] for j in range(groups)]
    to_plane = [
        [(d, d // owners * owners + (d % owners + 2 * s) % owners) for d in everyone] for s in range(planes)
    ]
    order = plane_order(planes)
    others = range(1, groups)

    turned, upstream, first_keep, first_send, chosen = first_blocks(
        row_counts, plan_now, plan_next, hidden_acts[0, 0], out_grads[0, 0], experts
    )
    now, later = chosen[0], chosen[1]

    mail = Mail()
    mail.send("first", first_send, to_core)
    rest_keep, rest_send = rest_blocks(mail.hold(turned, ["first"]), upstream, groups, planes)
    mail.send("rest", rest_send, to_core)
    keep, held = {}, {}
    for n, s in enumerate(order):
        keep[s], held[s] = (rest_keep[n - 1], mail["rest"][n - 1]) if n else (first_keep[0], mail["first"][0])
    window = 5
    names = []
    for n, s in enumerate(order):
        names += [(s, j) for j in others]
        if n and order[n - 1]:
            names.append(("sum", order[n - 1]))

    def start(s, j, value, pairs):
        at = names.index((s, j))
        mail.send((s, j), value, pairs, names[at - window : at - window + 1] if at >= window else ())

    def plane_sum(s):
        total = jnp.zeros((experts, rows, cols), jnp.float32)
        for j in range(groups):
            block = mail[s, j] if j else jnp.stack([keep[s][0], held[s][0]])
            for i in range(2):
                total = total + now[2 * j + i][:, None] * block[i].astype(jnp.float32)
        return total

    for name in names:
        if name[0] == "sum":
            s = name[1]
            start("sum", s, plane_sum(s).astype(jnp.bfloat16), to_plane[s])
        else:
            s, j = name
            start(s, j, jnp.stack([keep[s][j], held[s][j]]), to_group[j])
    grad_sum = plane_sum(0)
    for s in order:
        if s:
            grad_sum = grad_sum + mail["sum", s].astype(jnp.float32)

    master_new, moment_one_new, moment_two_new = adam(grad_sum, master, moment_one, moment_two)
    rounded = master_new.astype(jnp.bfloat16)

    def chosen_blocks(shard):
        shard = shard.astype(jnp.float32)
        return [
            jnp.stack(
                [jnp.sum(later[2 * j + i][:, None] * shard, axis=0).astype(jnp.bfloat16) for i in range(2)]
            )
            for j in range(groups)
        ]

    def in_order(blocks):
        for bit in range(groups.bit_length() - 1):
            swap = (group >> bit) & 1 == 1
            blocks = [jnp.where(swap, blocks[m ^ (1 << bit)], blocks[m]) for m in range(groups)]
        return jnp.concatenate(blocks, axis=-1)

    back = order[::-1]
    own = {}
    mail = Mail()

    def spread(n):
        s, before = back[n], back[n - 1]
        shard = mail.hold(mail["shard", s], [(before, 1)]) if s else rounded
        own[s], *blocks = chosen_blocks(shard)
        for j, block in enumerate(blocks, 1):
            mail.send((s, j), block, to_group[j], [(before, j)] if s and j > 1 else [])

    def pass_on(n):
        s = back[n]
        blocks = jnp.stack([own[s][1]] + [mail[s, j][1] for j in others])
        mail.send(("core", s), blocks, to_core)

    def shards(n, after):
        s = back[n]
        mail.send(("shard", s), rounded, to_plane[s], after)

    last = planes - 1
    for n in range(planes):
        if n == 0:
            shards(1, [])
            spread(0)
            if last >= 2:
                shards(2, [])
            if last >= 3:
                shards(3, [("shard", back[1])])
        else:
            spread(n)
            if n + 3 <= last:
                shards(n + 3, [("shard", back[n + 1])])
        pass_on(n)

    replica = jnp.zeros((planes, 2, rows, groups * cols), jnp.bfloat16)
    for s in back:
        mine = in_order([own[s][0]] + [mail[s, j][0] for j in others])
        other = in_order([mail["core", s][j] for j in range(groups)])
        both = jnp.stack([jnp.where(core == 0, mine, other), jnp.where(core == 0, other, mine)])
        replica = lax.dynamic_update_index_in_dim(replica, both, lax.rem(plane - s + planes, planes), 0)
    replica = replica.reshape(2 * planes * rows, groups * cols)
    return (master_new, moment_one_new, moment_two_new, replica[None, None])


def per_device_whole(
    hidden_acts, out_grads, row_counts, plan_now, plan_next, master, moment_one, moment_two
):
    ex_count = lax.axis_size("expert")
    dp_index = lax.axis_index("dp")
    experts = master.shape[0]
    piece_rows = master.shape[1]
    hidden = hidden_acts[0, 0]
    upstream = out_grads[0, 0]
    width = upstream.shape[1]
    row_index = jnp.arange(hidden.shape[0], dtype=jnp.int32)
    row_mask = (row_index < row_counts[0, 0]).astype(hidden.dtype)[:, None]
    partial_value = lax.dot_general(
        hidden * row_mask, upstream, (((0,), (0,)), ((), ())), preferred_element_type=jnp.float32
    ).astype(jnp.bfloat16)
    expert_ids = jnp.arange(experts, dtype=jnp.int32)
    pieces = lax.all_to_all(
        partial_value.reshape(ex_count, piece_rows, width),
        "expert",
        split_axis=0,
        concat_axis=0,
        tiled=True,
    )
    sender_ids = lax.dynamic_index_in_dim(plan_now, dp_index, 0, keepdims=False)
    onehot = (sender_ids[None, :] == expert_ids[:, None]).astype(jnp.bfloat16)
    totals = jnp.einsum("es,srd->erd", onehot, pieces, preferred_element_type=jnp.float32)
    grad_sum = lax.psum_scatter(
        totals.astype(jnp.bfloat16), "dp", scatter_dimension=2, tiled=True
    ).astype(jnp.float32)
    master_new, moment_one_new, moment_two_new = adam(grad_sum, master, moment_one, moment_two)
    rounded = master_new.astype(jnp.bfloat16)
    full_cols = lax.all_gather(rounded, "dp", axis=2, tiled=True)
    targets = lax.dynamic_index_in_dim(plan_next, dp_index, 0, keepdims=False)
    outgoing = jnp.take(full_cols, targets, axis=0)
    incoming = lax.all_to_all(outgoing, "expert", split_axis=0, concat_axis=0, tiled=True)
    replica = incoming.reshape(ex_count * piece_rows, width)
    return (master_new, moment_one_new, moment_two_new, replica[None, None])


def per_device(hidden_acts, out_grads, row_counts, plan_now, plan_next, master, *moments):
    groups = lax.axis_size("dp")
    owners = lax.axis_size("expert")
    experts, rows, cols = master.shape
    few = experts <= 2 * groups and owners <= 8
    even = owners % 2 == 0 and groups & (groups - 1) == 0 and rows % 16 == 0 and cols % 128 == 0
    body = per_device_planes if few and even else per_device_whole
    return body(hidden_acts, out_grads, row_counts, plan_now, plan_next, master, *moments)


def solution(mesh):
    return jax.shard_map(
        per_device,
        mesh=mesh,
        in_specs=(
            P("dp", "expert", None, None),
            P("dp", "expert", None, None),
            P("dp", "expert"),
            P(),
            P(),
            P(None, "expert", "dp"),
            P(None, "expert", "dp"),
            P(None, "expert", "dp"),
        ),
        out_specs=(
            P(None, "expert", "dp"),
            P(None, "expert", "dp"),
            P(None, "expert", "dp"),
            P("dp", "expert", None, None),
        ),
        check_vma=False,
    )
```

```python
import jax
import jax.numpy as jnp
from jax import lax
from jax.experimental import pallas as pl
from jax.experimental.pallas import tpu as pltpu
from jax.sharding import PartitionSpec as P

beta_one = 0.9
beta_two = 0.999
learn_rate = 0.1
epsilon = 1e-08
first_fix = 1.0 - beta_one**10
second_fix = 1.0 - beta_two**10

AXES = ("dp", "expert")

SUM_TIES = {
    (1, 3): [(0, 1)],
    ("sum", 0): [(0, 2)],
    ("sum", 1): [(1, 3)],
    (3, 1): [("sum", 0)],
    (3, 2): [(0, 1), (0, 3)],
    (3, 3): [(2, 2)],
    ("sum", 2): [(2, 3)],
    "rest": [(0, 2)],
    (1, 1): [(0, 2)],
}
SPREAD_TIES = {
    ("choose", 1): [(0, 2)],
    (1, 2): [(0, 2)],
    ("choose", 2): [(1, 3)],
    (2, 2): [("core", 0)],
    ("choose", 3): [(2, 3), ("core", 0)],
    (3, 2): [(1, 3)],
    (3, 3): [(2, 3)],
    ("shard", 2): [(0, 1)],
    ("core", 1): [(2, 3), (2, 2)],
    ("core", 0): [("shard", 2)],
    (2, 1): [("core", 0)],
    ("core", 2): [(3, 3)],
    ("core", 3): [(3, 1)],
}


def adam(grad_sum, master, moment_one, moment_two):
    moment_one_new = beta_one * moment_one + (1.0 - beta_one) * grad_sum
    moment_two_new = beta_two * moment_two + (1.0 - beta_two) * grad_sum * grad_sum
    master_new = master - learn_rate * (moment_one_new / first_fix) / (
        jnp.sqrt(moment_two_new / second_fix) + epsilon
    )
    return master_new, moment_one_new, moment_two_new


PLANE_ORDER = (2, 3, 1, 0)


def store_blocks(product, even_core, rows, at, j, keep_ref, send_ref):
    even, odd = product[:rows], product[rows:]
    keep_ref[at, j] = jnp.where(even_core, even, odd).astype(keep_ref.dtype)
    send_ref[at, j] = jnp.where(even_core, odd, even).astype(send_ref.dtype)


def first_kernel(
    count_ref, now_hbm, next_hbm, hidden_hbm, upstream_hbm, turned_ref, upstream_ref, keep_ref, send_ref,
    chosen_ref, hidden_ref, now_ref, next_ref, sems, small_sems,
):
    tokens, inner = hidden_ref.shape
    lead, groups, rows, cols = keep_ref.shape
    planes = inner // (2 * rows)
    parts = sems.shape[1]
    part = tokens // parts
    group, owner = lax.axis_index("dp"), lax.axis_index("expert")
    plane, core = owner >> 1, owner & 1

    smalls = [
        pltpu.make_async_copy(source, target, small_sems.at[n])
        for n, (source, target) in enumerate(((now_hbm, now_ref), (next_hbm, next_ref)))
    ]
    for copy in smalls:
        copy.start()
    copies = []
    for n in range(parts):
        at = pl.ds(n * part, part)
        copies.append(
            [
                pltpu.make_async_copy(hidden_hbm.at[at], hidden_ref.at[at], sems.at[0, n]),
                pltpu.make_async_copy(upstream_hbm.at[at], upstream_ref.at[at], sems.at[1, n]),
            ]
        )
    for kind in range(2):
        for copy in copies:
            copy[kind].start()

    for copy in smalls:
        copy.wait()
    names = lax.broadcasted_iota(jnp.int32, chosen_ref.shape[2:], 0)
    for n, plan_ref in enumerate((now_ref, next_ref)):
        for near in range(2 * groups):
            named = plan_ref[group ^ (near // 2), 2 * plane + (core ^ (near % 2))]
            chosen_ref[n, near] = jnp.where(names == named, 1.0, 0.0)

    for n in range(parts):
        copies[n][0].wait()
        hidden = hidden_ref[n * part : (n + 1) * part]
        live = lax.broadcasted_iota(jnp.int32, hidden.shape, 0) < count_ref[0, 0] - n * part
        hidden = jnp.where(live, hidden, jnp.zeros_like(hidden)).T
        for m, s in enumerate(PLANE_ORDER):
            for p in range(planes):

                @pl.when(plane ^ s == p)
                def put():
                    turned_ref[2 * rows * m : 2 * rows * (m + 1), n * part : (n + 1) * part] = hidden[
                        2 * rows * p : 2 * rows * (p + 1)
                    ]
    for n in range(parts):
        copies[n][1].wait()

    def columns(j, carry):
        at = pl.ds(pl.multiple_of((group ^ j) * cols, cols), cols)
        product = jnp.dot(
            turned_ref[: 2 * rows * lead], upstream_ref[:, at], preferred_element_type=jnp.float32
        )
        for n in range(lead):
            part = product[2 * rows * n : 2 * rows * (n + 1)]
            store_blocks(part, core == 0, rows, n, j, keep_ref, send_ref)
        return carry

    lax.fori_loop(0, groups, columns, 0)


def rest_kernel(turned_ref, upstream_ref, keep_ref, send_ref):
    rest, groups, rows, cols = keep_ref.shape
    group, core = lax.axis_index("dp"), lax.axis_index("expert") & 1

    def columns(j, carry):
        at = pl.ds(pl.multiple_of((group ^ j) * cols, cols), cols)
        product = jnp.dot(
            turned_ref[-2 * rows * rest :], upstream_ref[:, at], preferred_element_type=jnp.float32
        )
        for n in range(rest):
            part = product[2 * rows * n : 2 * rows * (n + 1)]
            store_blocks(part, core == 0, rows, n, j, keep_ref, send_ref)
        return carry

    lax.fori_loop(0, groups, columns, 0)


def first_blocks(counts, plan_now, plan_next, hidden, upstream, experts, lead):
    groups, owners = plan_now.shape
    planes = owners // 2
    plan_now, plan_next, hidden, upstream = [
        pltpu.with_memory_space_constraint(array, pltpu.HBM)
        for array in (plan_now, plan_next, hidden, upstream)
    ]
    tokens, inner = hidden.shape
    width = upstream.shape[1]
    cols = width // groups
    rows = inner // owners
    parts = 4 if tokens % 512 == 0 else 1
    hbm = pl.BlockSpec(memory_space=pltpu.HBM)
    vmem = pl.BlockSpec(memory_space=pltpu.VMEM)

    def blocks(n):
        return jax.ShapeDtypeStruct((n, groups, rows, cols), jnp.bfloat16)

    turned, copied, keep, send, chosen = pl.pallas_call(
        first_kernel,
        in_specs=[pl.BlockSpec(memory_space=pltpu.SMEM)] + [hbm] * 4,
        out_specs=[vmem] * 5,
        out_shape=[
            jax.ShapeDtypeStruct((inner, tokens), jnp.bfloat16),
            jax.ShapeDtypeStruct((tokens, width), jnp.bfloat16),
            blocks(lead),
            blocks(lead),
            jax.ShapeDtypeStruct((2, 2 * groups, experts, cols), jnp.float32),
        ],
        scratch_shapes=[
            pltpu.VMEM((tokens, inner), jnp.bfloat16),
            pltpu.SMEM(plan_now.shape, jnp.int32),
            pltpu.SMEM(plan_next.shape, jnp.int32),
            pltpu.SemaphoreType.DMA((2, parts)),
            pltpu.SemaphoreType.DMA((2,)),
        ],
        compiler_params=pltpu.CompilerParams(vmem_limit_bytes=24 * 2**20),
        cost_estimate=pl.CostEstimate(
            flops=4 * tokens * rows * lead * width,
            bytes_accessed=2 * (tokens * inner + tokens * width),
            transcendentals=0,
        ),
        name="first_blocks",
    )(counts, plan_now, plan_next, hidden, upstream)
    return turned, copied, keep, send, chosen


def rest_blocks(turned, upstream, groups, planes, rest):
    tokens, width = upstream.shape
    inner = turned.shape[0]
    cols = width // groups
    rows = inner // (2 * planes)
    vmem = pl.BlockSpec(memory_space=pltpu.VMEM)
    out = jax.ShapeDtypeStruct((rest, groups, rows, cols), jnp.bfloat16)
    return pl.pallas_call(
        rest_kernel,
        in_specs=[vmem, vmem],
        out_specs=[vmem, vmem],
        out_shape=[out, out],
        compiler_params=pltpu.CompilerParams(vmem_limit_bytes=24 * 2**20),
        cost_estimate=pl.CostEstimate(
            flops=4 * tokens * rows * rest * width,
            bytes_accessed=4 * rows * rest * width,
            transcendentals=0,
        ),
        name="rest_blocks",
    )(turned, upstream)


class Mail:
    def __init__(self, ties):
        self.ties = ties
        self.arrived = {}

    def send(self, name, value, pairs):
        self.arrived[name] = lax.ppermute(self.hold(name, value), AXES, pairs)

    def hold(self, name, value):
        after = [self.arrived[n] for n in self.ties.get(name, ()) if n in self.arrived]
        return lax.optimization_barrier((value, *after))[0] if after else value

    def __getitem__(self, name):
        return self.arrived[name]


def per_device_planes(
    hidden_acts, out_grads, row_counts, plan_now, plan_next, master, moment_one, moment_two
):
    groups = lax.axis_size("dp")
    owners = lax.axis_size("expert")
    planes = owners // 2
    group = lax.axis_index("dp")
    owner = lax.axis_index("expert")
    plane, core = owner >> 1, owner & 1
    experts, rows, cols = master.shape

    everyone = range(groups * owners)
    to_core = [(d, d ^ 1) for d in everyone]
    to_group = [[(d, d ^ (j * owners)) for d in everyone] for j in range(groups)]
    to_plane = [[(d, d ^ 2 * s) for d in everyone] for s in range(planes)]
    others = range(1, groups)
    lead = 2

    turned, upstream, first_keep, first_send, chosen = first_blocks(
        row_counts, plan_now, plan_next, hidden_acts[0, 0], out_grads[0, 0], experts, lead
    )
    now, later = chosen[0], chosen[1]

    mail = Mail(SUM_TIES)
    mail.send("first", first_send, to_core)
    keep, held = [[blocks[n] for n in range(lead)] for blocks in (first_keep, mail["first"])]

    def plane_sum(n):
        total = jnp.zeros((experts, rows, cols), jnp.float32)
        for j in range(groups):
            block = mail[n, j] if j else jnp.stack([keep[n][0], held[n][0]])
            for i in range(2):
                total = total + now[2 * j + i][:, None] * block[i].astype(jnp.float32)
        return total

    for n in range(planes):
        if n == lead:
            rest_keep, rest_send = rest_blocks(
                mail.hold("rest", turned), upstream, groups, planes, planes - lead
            )
            for m in range(planes - lead):
                mail.send(("other", m), rest_send[m], to_core)
                keep.append(rest_keep[m])
                held.append(mail["other", m])
        for j in others:
            mail.send((n, j), jnp.stack([keep[n][j], held[n][j]]), to_group[j])
        if n:
            total = plane_sum(n - 1)
            if n == 2:
                total = total + mail["sum", 0].astype(jnp.float32)
            mail.send(("sum", n - 1), total.astype(jnp.bfloat16), to_plane[3 if n == 2 else 1])
    grad_sum = plane_sum(planes - 1)
    for n in range(1, planes - 1):
        grad_sum = grad_sum + mail["sum", n].astype(jnp.float32)

    master_new, moment_one_new, moment_two_new = adam(grad_sum, master, moment_one, moment_two)
    rounded = master_new.astype(jnp.bfloat16)

    def chosen_blocks(shard):
        shard = shard.astype(jnp.float32)
        return [
            jnp.stack(
                [jnp.sum(later[2 * j + i][:, None] * shard, axis=0).astype(jnp.bfloat16) for i in range(2)]
            )
            for j in range(groups)
        ]

    def in_order(blocks):
        for bit in range(groups.bit_length() - 1):
            swap = (group >> bit) & 1 == 1
            blocks = [jnp.where(swap, blocks[m ^ (1 << bit)], blocks[m]) for m in range(groups)]
        return jnp.concatenate(blocks, axis=-1)

    back = PLANE_ORDER[::-1]
    own = {}
    mail = Mail(SPREAD_TIES)

    def send_shard(n):
        mail.send(("shard", n), mail["shard", 2] if n == 3 else rounded, to_plane[3 if n == 2 else 1])

    def pass_on(n):
        blocks = jnp.stack([own[n][1]] + [mail[n, j][1] for j in others])
        mail.send(("core", n), blocks, to_core)

    send_shard(1)
    for n in range(planes):
        own[n], *blocks = chosen_blocks(mail.hold(("choose", n), mail["shard", n]) if n else rounded)
        for j, block in enumerate(blocks, 1):
            mail.send((n, j), block, to_group[j])
        if n == 0:
            for m in range(2, planes):
                send_shard(m)
        else:
            pass_on(n - 1)
    pass_on(planes - 1)

    replica = jnp.zeros((planes, 2, rows, groups * cols), jnp.bfloat16)
    for n, s in enumerate(back):
        mine = in_order([own[n][0]] + [mail[n, j][0] for j in others])
        other = in_order([mail["core", n][j] for j in range(groups)])
        both = jnp.stack([jnp.where(core == 0, mine, other), jnp.where(core == 0, other, mine)])
        replica = lax.dynamic_update_index_in_dim(replica, both, plane ^ s, 0)
    replica = replica.reshape(2 * planes * rows, groups * cols)
    return (master_new, moment_one_new, moment_two_new, replica[None, None])


def per_device_whole(
    hidden_acts, out_grads, row_counts, plan_now, plan_next, master, moment_one, moment_two
):
    ex_count = lax.axis_size("expert")
    dp_index = lax.axis_index("dp")
    experts = master.shape[0]
    piece_rows = master.shape[1]
    hidden = hidden_acts[0, 0]
    upstream = out_grads[0, 0]
    width = upstream.shape[1]
    row_index = jnp.arange(hidden.shape[0], dtype=jnp.int32)
    row_mask = (row_index < row_counts[0, 0]).astype(hidden.dtype)[:, None]
    partial_value = lax.dot_general(
        hidden * row_mask, upstream, (((0,), (0,)), ((), ())), preferred_element_type=jnp.float32
    ).astype(jnp.bfloat16)
    expert_ids = jnp.arange(experts, dtype=jnp.int32)
    pieces = lax.all_to_all(
        partial_value.reshape(ex_count, piece_rows, width),
        "expert",
        split_axis=0,
        concat_axis=0,
        tiled=True,
    )
    sender_ids = lax.dynamic_index_in_dim(plan_now, dp_index, 0, keepdims=False)
    onehot = (sender_ids[None, :] == expert_ids[:, None]).astype(jnp.bfloat16)
    totals = jnp.einsum("es,srd->erd", onehot, pieces, preferred_element_type=jnp.float32)
    grad_sum = lax.psum_scatter(
        totals.astype(jnp.bfloat16), "dp", scatter_dimension=2, tiled=True
    ).astype(jnp.float32)
    master_new, moment_one_new, moment_two_new = adam(grad_sum, master, moment_one, moment_two)
    rounded = master_new.astype(jnp.bfloat16)
    full_cols = lax.all_gather(rounded, "dp", axis=2, tiled=True)
    targets = lax.dynamic_index_in_dim(plan_next, dp_index, 0, keepdims=False)
    outgoing = jnp.take(full_cols, targets, axis=0)
    incoming = lax.all_to_all(outgoing, "expert", split_axis=0, concat_axis=0, tiled=True)
    replica = incoming.reshape(ex_count * piece_rows, width)
    return (master_new, moment_one_new, moment_two_new, replica[None, None])


def per_device(hidden_acts, out_grads, row_counts, plan_now, plan_next, master, *moments):
    groups = lax.axis_size("dp")
    owners = lax.axis_size("expert")
    experts, rows, cols = master.shape
    few = experts <= 2 * groups and owners == 2 * len(PLANE_ORDER)
    even = groups & (groups - 1) == 0 and rows % 16 == 0 and cols % 128 == 0
    body = per_device_planes if few and even else per_device_whole
    return body(hidden_acts, out_grads, row_counts, plan_now, plan_next, master, *moments)


def solution(mesh):
    return jax.shard_map(
        per_device,
        mesh=mesh,
        in_specs=(
            P("dp", "expert", None, None),
            P("dp", "expert", None, None),
            P("dp", "expert"),
            P(),
            P(),
            P(None, "expert", "dp"),
            P(None, "expert", "dp"),
            P(None, "expert", "dp"),
        ),
        out_specs=(
            P(None, "expert", "dp"),
            P(None, "expert", "dp"),
            P(None, "expert", "dp"),
            P("dp", "expert", None, None),
        ),
        check_vma=False,
    )
```

```python
import jax
import jax.numpy as jnp
from jax import lax
from jax.experimental import pallas as pl
from jax.experimental.pallas import tpu as pltpu
from jax.sharding import PartitionSpec as P

beta_one = 0.9
beta_two = 0.999
learn_rate = 0.1
epsilon = 1e-08
first_fix = 1.0 - beta_one**10
second_fix = 1.0 - beta_two**10

AXES = ("dp", "expert")

SUM_TIES = {
    (1, 3): [(0, 1)],
    ("sum", 0): [(0, 2)],
    (2, 1): [("other", 1)],
    (2, 3): [("other", 1), (1, 3)],
    ("sum", 1): [(1, 3)],
    (3, 1): [("sum", 0)],
    (3, 2): [(0, 1), (0, 3)],
    (3, 3): [(2, 2)],
    ("sum", 2): [(2, 3)],
    "rest": [(0, 2)],
    (1, 1): [(0, 3)],
}
SPREAD_TIES = {
    ("choose", 1): [(0, 1)],
    (1, 2): [(0, 2)],
    (1, 3): [(0, 3)],
    ("choose", 2): [(1, 3)],
    (2, 2): [("core", 0)],
    ("choose", 3): [(2, 3), ("core", 0)],
    (3, 2): [(1, 3)],
    (3, 3): [(2, 3)],
    ("shard", 2): [(0, 1)],
    ("core", 1): [(2, 3), (2, 2)],
    ("core", 0): [("shard", 2)],
    (2, 1): [("core", 0)],
    ("core", 2): [(3, 1)],
    ("core", 3): [(3, 1)],
    (1, 1): [(0, 1), (0, 2)],
}


def adam(grad_sum, master, moment_one, moment_two):
    moment_one_new = beta_one * moment_one + (1.0 - beta_one) * grad_sum
    moment_two_new = beta_two * moment_two + (1.0 - beta_two) * grad_sum * grad_sum
    master_new = master - learn_rate * (moment_one_new / first_fix) / (
        jnp.sqrt(moment_two_new / second_fix) + epsilon
    )
    return master_new, moment_one_new, moment_two_new


PLANE_ORDER = (2, 3, 1, 0)


def store_blocks(product, even_core, rows, at, j, keep_ref, send_ref):
    even, odd = product[:rows], product[rows:]
    keep_ref[at, j] = jnp.where(even_core, even, odd).astype(keep_ref.dtype)
    send_ref[at, j] = jnp.where(even_core, odd, even).astype(send_ref.dtype)


def first_kernel(
    count_ref, now_hbm, next_hbm, hidden_hbm, upstream_hbm, turned_ref, upstream_ref, keep_ref, send_ref,
    chosen_ref, hidden_ref, now_ref, next_ref, sems, small_sems,
):
    tokens, inner = hidden_ref.shape
    lead, groups, rows, cols = keep_ref.shape
    planes = inner // (2 * rows)
    parts = sems.shape[1]
    part = tokens // parts
    group, owner = lax.axis_index("dp"), lax.axis_index("expert")
    plane, core = owner >> 1, owner & 1

    smalls = [
        pltpu.make_async_copy(source, target, small_sems.at[n])
        for n, (source, target) in enumerate(((now_hbm, now_ref), (next_hbm, next_ref)))
    ]
    for copy in smalls:
        copy.start()
    copies = []
    for n in range(parts):
        at = pl.ds(n * part, part)
        copies.append(
            [
                pltpu.make_async_copy(hidden_hbm.at[at], hidden_ref.at[at], sems.at[0, n]),
                pltpu.make_async_copy(upstream_hbm.at[at], upstream_ref.at[at], sems.at[1, n]),
            ]
        )
    for kind in range(2):
        for copy in copies:
            copy[kind].start()

    for copy in smalls:
        copy.wait()
    names = lax.broadcasted_iota(jnp.int32, chosen_ref.shape[2:], 0)
    for n, plan_ref in enumerate((now_ref, next_ref)):
        for near in range(2 * groups):
            named = plan_ref[group ^ (near // 2), 2 * plane + (core ^ (near % 2))]
            chosen_ref[n, near] = jnp.where(names == named, 1.0, 0.0)

    for n in range(parts):
        copies[n][0].wait()
        hidden = hidden_ref[n * part : (n + 1) * part]
        live = lax.broadcasted_iota(jnp.int32, hidden.shape, 0) < count_ref[0, 0] - n * part
        hidden = jnp.where(live, hidden, jnp.zeros_like(hidden)).T
        for m, s in enumerate(PLANE_ORDER):
            for p in range(planes):

                @pl.when(plane ^ s == p)
                def put():
                    turned_ref[2 * rows * m : 2 * rows * (m + 1), n * part : (n + 1) * part] = hidden[
                        2 * rows * p : 2 * rows * (p + 1)
                    ]
    for n in range(parts):
        copies[n][1].wait()

    def columns(j, carry):
        at = pl.ds(pl.multiple_of((group ^ j) * cols, cols), cols)
        product = jnp.dot(
            turned_ref[: 2 * rows * lead], upstream_ref[:, at], preferred_element_type=jnp.float32
        )
        for n in range(lead):
            part = product[2 * rows * n : 2 * rows * (n + 1)]
            store_blocks(part, core == 0, rows, n, j, keep_ref, send_ref)
        return carry

    lax.fori_loop(0, groups, columns, 0)


def rest_kernel(turned_ref, upstream_ref, keep_ref, send_ref):
    rest, groups, rows, cols = keep_ref.shape
    group, core = lax.axis_index("dp"), lax.axis_index("expert") & 1

    def columns(j, carry):
        at = pl.ds(pl.multiple_of((group ^ j) * cols, cols), cols)
        product = jnp.dot(
            turned_ref[-2 * rows * rest :], upstream_ref[:, at], preferred_element_type=jnp.float32
        )
        for n in range(rest):
            part = product[2 * rows * n : 2 * rows * (n + 1)]
            store_blocks(part, core == 0, rows, n, j, keep_ref, send_ref)
        return carry

    lax.fori_loop(0, groups, columns, 0)


def first_blocks(counts, plan_now, plan_next, hidden, upstream, experts, lead):
    groups, owners = plan_now.shape
    planes = owners // 2
    plan_now, plan_next, hidden, upstream = [
        pltpu.with_memory_space_constraint(array, pltpu.HBM)
        for array in (plan_now, plan_next, hidden, upstream)
    ]
    tokens, inner = hidden.shape
    width = upstream.shape[1]
    cols = width // groups
    rows = inner // owners
    parts = 4 if tokens % 512 == 0 else 1
    hbm = pl.BlockSpec(memory_space=pltpu.HBM)
    vmem = pl.BlockSpec(memory_space=pltpu.VMEM)

    def blocks(n):
        return jax.ShapeDtypeStruct((n, groups, rows, cols), jnp.bfloat16)

    turned, copied, keep, send, chosen = pl.pallas_call(
        first_kernel,
        in_specs=[pl.BlockSpec(memory_space=pltpu.SMEM)] + [hbm] * 4,
        out_specs=[vmem] * 5,
        out_shape=[
            jax.ShapeDtypeStruct((inner, tokens), jnp.bfloat16),
            jax.ShapeDtypeStruct((tokens, width), jnp.bfloat16),
            blocks(lead),
            blocks(lead),
            jax.ShapeDtypeStruct((2, 2 * groups, experts, cols), jnp.float32),
        ],
        scratch_shapes=[
            pltpu.VMEM((tokens, inner), jnp.bfloat16),
            pltpu.SMEM(plan_now.shape, jnp.int32),
            pltpu.SMEM(plan_next.shape, jnp.int32),
            pltpu.SemaphoreType.DMA((2, parts)),
            pltpu.SemaphoreType.DMA((2,)),
        ],
        compiler_params=pltpu.CompilerParams(vmem_limit_bytes=24 * 2**20),
        cost_estimate=pl.CostEstimate(
            flops=4 * tokens * rows * lead * width,
            bytes_accessed=2 * (tokens * inner + tokens * width),
            transcendentals=0,
        ),
        name="first_blocks",
    )(counts, plan_now, plan_next, hidden, upstream)
    return turned, copied, keep, send, chosen


def rest_blocks(turned, upstream, groups, planes, rest):
    tokens, width = upstream.shape
    inner = turned.shape[0]
    cols = width // groups
    rows = inner // (2 * planes)
    vmem = pl.BlockSpec(memory_space=pltpu.VMEM)
    out = jax.ShapeDtypeStruct((rest, groups, rows, cols), jnp.bfloat16)
    return pl.pallas_call(
        rest_kernel,
        in_specs=[vmem, vmem],
        out_specs=[vmem, vmem],
        out_shape=[out, out],
        compiler_params=pltpu.CompilerParams(vmem_limit_bytes=24 * 2**20),
        cost_estimate=pl.CostEstimate(
            flops=4 * tokens * rows * rest * width,
            bytes_accessed=4 * rows * rest * width,
            transcendentals=0,
        ),
        name="rest_blocks",
    )(turned, upstream)


class Mail:
    def __init__(self, ties):
        self.ties = ties
        self.arrived = {}

    def send(self, name, value, pairs):
        self.arrived[name] = lax.ppermute(self.hold(name, value), AXES, pairs)

    def hold(self, name, value):
        after = [self.arrived[n] for n in self.ties.get(name, ()) if n in self.arrived]
        return lax.optimization_barrier((value, *after))[0] if after else value

    def __getitem__(self, name):
        return self.arrived[name]


def per_device_planes(
    hidden_acts, out_grads, row_counts, plan_now, plan_next, master, moment_one, moment_two
):
    groups = lax.axis_size("dp")
    owners = lax.axis_size("expert")
    planes = owners // 2
    group = lax.axis_index("dp")
    owner = lax.axis_index("expert")
    plane, core = owner >> 1, owner & 1
    experts, rows, cols = master.shape

    everyone = range(groups * owners)
    to_core = [(d, d ^ 1) for d in everyone]
    to_group = [[(d, d ^ (j * owners)) for d in everyone] for j in range(groups)]
    to_plane = [[(d, d ^ 2 * s) for d in everyone] for s in range(planes)]
    others = range(1, groups)
    lead = 3

    turned, upstream, first_keep, first_send, chosen = first_blocks(
        row_counts, plan_now, plan_next, hidden_acts[0, 0], out_grads[0, 0], experts, lead
    )
    now, later = chosen[0], chosen[1]

    mail = Mail(SUM_TIES)
    mail.send("first", first_send, to_core)
    keep, held = [[blocks[n] for n in range(lead)] for blocks in (first_keep, mail["first"])]

    def plane_sum(n):
        total = jnp.zeros((experts, rows, cols), jnp.float32)
        for j in range(groups):
            block = mail[n, j] if j else jnp.stack([keep[n][0], held[n][0]])
            for i in range(2):
                total = total + now[2 * j + i][:, None] * block[i].astype(jnp.float32)
        return total

    for n in range(planes):
        if n == lead:
            rest_keep, rest_send = rest_blocks(
                mail.hold("rest", turned), upstream, groups, planes, planes - lead
            )
            for m in range(planes - lead):
                mail.send(("other", m), rest_send[m], to_core)
                keep.append(rest_keep[m])
                held.append(mail["other", m])
        for j in others:
            mail.send((n, j), jnp.stack([keep[n][j], held[n][j]]), to_group[j])
        if n:
            total = plane_sum(n - 1)
            if n == 2:
                total = total + mail["sum", 0].astype(jnp.float32)
            mail.send(("sum", n - 1), total.astype(jnp.bfloat16), to_plane[3 if n == 2 else 1])
    grad_sum = plane_sum(planes - 1)
    for n in range(1, planes - 1):
        grad_sum = grad_sum + mail["sum", n].astype(jnp.float32)

    master_new, moment_one_new, moment_two_new = adam(grad_sum, master, moment_one, moment_two)
    rounded = master_new.astype(jnp.bfloat16)

    def chosen_blocks(shard):
        shard = shard.astype(jnp.float32)
        return [
            jnp.stack(
                [jnp.sum(later[2 * j + i][:, None] * shard, axis=0).astype(jnp.bfloat16) for i in range(2)]
            )
            for j in range(groups)
        ]

    def in_order(blocks):
        for bit in range(groups.bit_length() - 1):
            swap = (group >> bit) & 1 == 1
            blocks = [jnp.where(swap, blocks[m ^ (1 << bit)], blocks[m]) for m in range(groups)]
        return jnp.concatenate(blocks, axis=-1)

    back = PLANE_ORDER[::-1]
    own = {}
    mail = Mail(SPREAD_TIES)

    def send_shard(n):
        mail.send(("shard", n), mail["shard", 2] if n == 3 else rounded, to_plane[3 if n == 2 else 1])

    def pass_on(n):
        blocks = jnp.stack([own[n][1]] + [mail[n, j][1] for j in others])
        mail.send(("core", n), blocks, to_core)

    send_shard(1)
    for n in range(planes):
        own[n], *blocks = chosen_blocks(mail.hold(("choose", n), mail["shard", n]) if n else rounded)
        for j, block in enumerate(blocks, 1):
            mail.send((n, j), block, to_group[j])
        if n == 0:
            for m in range(2, planes):
                send_shard(m)
        else:
            pass_on(n - 1)
    pass_on(planes - 1)

    replica = jnp.zeros((planes, 2, rows, groups * cols), jnp.bfloat16)
    for n, s in enumerate(back):
        mine = in_order([own[n][0]] + [mail[n, j][0] for j in others])
        other = in_order([mail["core", n][j] for j in range(groups)])
        both = jnp.stack([jnp.where(core == 0, mine, other), jnp.where(core == 0, other, mine)])
        replica = lax.dynamic_update_index_in_dim(replica, both, plane ^ s, 0)
    replica = replica.reshape(2 * planes * rows, groups * cols)
    return (master_new, moment_one_new, moment_two_new, replica[None, None])


def per_device_whole(
    hidden_acts, out_grads, row_counts, plan_now, plan_next, master, moment_one, moment_two
):
    ex_count = lax.axis_size("expert")
    dp_index = lax.axis_index("dp")
    experts = master.shape[0]
    piece_rows = master.shape[1]
    hidden = hidden_acts[0, 0]
    upstream = out_grads[0, 0]
    width = upstream.shape[1]
    row_index = jnp.arange(hidden.shape[0], dtype=jnp.int32)
    row_mask = (row_index < row_counts[0, 0]).astype(hidden.dtype)[:, None]
    partial_value = lax.dot_general(
        hidden * row_mask, upstream, (((0,), (0,)), ((), ())), preferred_element_type=jnp.float32
    ).astype(jnp.bfloat16)
    expert_ids = jnp.arange(experts, dtype=jnp.int32)
    pieces = lax.all_to_all(
        partial_value.reshape(ex_count, piece_rows, width),
        "expert",
        split_axis=0,
        concat_axis=0,
        tiled=True,
    )
    sender_ids = lax.dynamic_index_in_dim(plan_now, dp_index, 0, keepdims=False)
    onehot = (sender_ids[None, :] == expert_ids[:, None]).astype(jnp.bfloat16)
    totals = jnp.einsum("es,srd->erd", onehot, pieces, preferred_element_type=jnp.float32)
    grad_sum = lax.psum_scatter(
        totals.astype(jnp.bfloat16), "dp", scatter_dimension=2, tiled=True
    ).astype(jnp.float32)
    master_new, moment_one_new, moment_two_new = adam(grad_sum, master, moment_one, moment_two)
    rounded = master_new.astype(jnp.bfloat16)
    full_cols = lax.all_gather(rounded, "dp", axis=2, tiled=True)
    targets = lax.dynamic_index_in_dim(plan_next, dp_index, 0, keepdims=False)
    outgoing = jnp.take(full_cols, targets, axis=0)
    incoming = lax.all_to_all(outgoing, "expert", split_axis=0, concat_axis=0, tiled=True)
    replica = incoming.reshape(ex_count * piece_rows, width)
    return (master_new, moment_one_new, moment_two_new, replica[None, None])


def per_device(hidden_acts, out_grads, row_counts, plan_now, plan_next, master, *moments):
    groups = lax.axis_size("dp")
    owners = lax.axis_size("expert")
    experts, rows, cols = master.shape
    few = experts <= 2 * groups and owners == 2 * len(PLANE_ORDER)
    even = groups & (groups - 1) == 0 and rows % 16 == 0 and cols % 128 == 0
    body = per_device_planes if few and even else per_device_whole
    return body(hidden_acts, out_grads, row_counts, plan_now, plan_next, master, *moments)


def solution(mesh):
    return jax.shard_map(
        per_device,
        mesh=mesh,
        in_specs=(
            P("dp", "expert", None, None),
            P("dp", "expert", None, None),
            P("dp", "expert"),
            P(),
            P(),
            P(None, "expert", "dp"),
            P(None, "expert", "dp"),
            P(None, "expert", "dp"),
        ),
        out_specs=(
            P(None, "expert", "dp"),
            P(None, "expert", "dp"),
            P(None, "expert", "dp"),
            P("dp", "expert", None, None),
        ),
        check_vma=False,
    )
```

```python
import jax
import jax.numpy as jnp
from jax import lax
from jax.experimental import pallas as pl
from jax.experimental.pallas import tpu as pltpu
from jax.sharding import PartitionSpec as P

beta_one = 0.9
beta_two = 0.999
learn_rate = 0.1
epsilon = 1e-08
first_fix = 1.0 - beta_one**10
second_fix = 1.0 - beta_two**10

AXES = ("dp", "expert")

SUM_TIES = {
    (1, 3): [(0, 1)],
    ("sum", 0): [(0, 2)],
    (2, 3): [(1, 3)],
    ("sum", 1): [(1, 3)],
    (3, 1): [("sum", 0)],
    (3, 2): [(0, 1), (0, 3)],
    (3, 3): [(2, 2)],
    ("sum", 2): [(2, 3)],
    "rest": [(0, 2)],
    (1, 1): [(0, 3)],
}
SPREAD_TIES = {
    ("choose", 1): [(0, 1)],
    (1, 2): [(0, 2)],
    (1, 3): [(0, 3)],
    ("choose", 2): [(1, 3)],
    (2, 2): [("core", 0)],
    ("choose", 3): [(2, 3), ("core", 0)],
    (3, 2): [(1, 3)],
    (3, 3): [(2, 3)],
    ("shard", 2): [(0, 1)],
    ("core", 1): [(2, 3), (2, 2)],
    ("core", 0): [("shard", 2)],
    (2, 1): [("core", 0)],
    ("core", 2): [(3, 1)],
    ("core", 3): [(3, 1)],
    (1, 1): [(0, 1), (0, 2)],
}


def adam(grad_sum, master, moment_one, moment_two):
    moment_one_new = beta_one * moment_one + (1.0 - beta_one) * grad_sum
    moment_two_new = beta_two * moment_two + (1.0 - beta_two) * grad_sum * grad_sum
    master_new = master - learn_rate * (moment_one_new / first_fix) / (
        jnp.sqrt(moment_two_new / second_fix) + epsilon
    )
    return master_new, moment_one_new, moment_two_new


PLANE_ORDER = (2, 3, 1, 0)


def store_blocks(product, even_core, rows, at, j, keep_ref, send_ref):
    even, odd = product[:rows], product[rows:]
    keep_ref[at, j] = jnp.where(even_core, even, odd).astype(keep_ref.dtype)
    send_ref[at, j] = jnp.where(even_core, odd, even).astype(send_ref.dtype)


def first_kernel(
    count_ref, now_hbm, next_hbm, hidden_hbm, upstream_hbm, turned_ref, upstream_ref, keep_ref, send_ref,
    chosen_ref, hidden_ref, now_ref, next_ref, sems, column_sems, small_sems,
):
    tokens, inner = hidden_ref.shape
    lead, groups, rows, cols = keep_ref.shape
    planes = inner // (2 * rows)
    parts = sems.shape[0]
    part = tokens // parts
    group, owner = lax.axis_index("dp"), lax.axis_index("expert")
    plane, core = owner >> 1, owner & 1

    smalls = [
        pltpu.make_async_copy(source, target, small_sems.at[n])
        for n, (source, target) in enumerate(((now_hbm, now_ref), (next_hbm, next_ref)))
    ]
    for copy in smalls:
        copy.start()
    copies = [
        pltpu.make_async_copy(
            hidden_hbm.at[pl.ds(n * part, part)], hidden_ref.at[pl.ds(n * part, part)], sems.at[n]
        )
        for n in range(parts)
    ]
    for copy in copies:
        copy.start()

    def column_copy(j):
        at = pl.ds(pl.multiple_of((group ^ j) * cols, cols), cols)
        return pltpu.make_async_copy(upstream_hbm.at[:, at], upstream_ref.at[:, at], column_sems.at[j])

    for j in range(groups):
        column_copy(j).start()

    for copy in smalls:
        copy.wait()
    names = lax.broadcasted_iota(jnp.int32, chosen_ref.shape[2:], 0)
    for n, plan_ref in enumerate((now_ref, next_ref)):
        for near in range(2 * groups):
            named = plan_ref[group ^ (near // 2), 2 * plane + (core ^ (near % 2))]
            chosen_ref[n, near] = jnp.where(names == named, 1.0, 0.0)

    for n in range(parts):
        copies[n].wait()
        hidden = hidden_ref[n * part : (n + 1) * part]
        live = lax.broadcasted_iota(jnp.int32, hidden.shape, 0) < count_ref[0, 0] - n * part
        hidden = jnp.where(live, hidden, jnp.zeros_like(hidden)).T
        for p in range(planes):
            position = sum(jnp.where(plane ^ s == p, m, 0) for m, s in enumerate(PLANE_ORDER))
            at = pl.ds(pl.multiple_of(position * 2 * rows, 2 * rows), 2 * rows)
            turned_ref[at, n * part : (n + 1) * part] = hidden[2 * rows * p : 2 * rows * (p + 1)]

    def columns(j, carry):
        column_copy(j).wait()
        at = pl.ds(pl.multiple_of((group ^ j) * cols, cols), cols)
        product = jnp.dot(
            turned_ref[: 2 * rows * lead], upstream_ref[:, at], preferred_element_type=jnp.float32
        )
        for n in range(lead):
            part = product[2 * rows * n : 2 * rows * (n + 1)]
            store_blocks(part, core == 0, rows, n, j, keep_ref, send_ref)
        return carry

    lax.fori_loop(0, groups, columns, 0)


def rest_kernel(turned_ref, upstream_ref, keep_ref, send_ref):
    rest, groups, rows, cols = keep_ref.shape
    group, core = lax.axis_index("dp"), lax.axis_index("expert") & 1

    def columns(j, carry):
        at = pl.ds(pl.multiple_of((group ^ j) * cols, cols), cols)
        product = jnp.dot(
            turned_ref[-2 * rows * rest :], upstream_ref[:, at], preferred_element_type=jnp.float32
        )
        for n in range(rest):
            part = product[2 * rows * n : 2 * rows * (n + 1)]
            store_blocks(part, core == 0, rows, n, j, keep_ref, send_ref)
        return carry

    lax.fori_loop(0, groups, columns, 0)


def first_blocks(counts, plan_now, plan_next, hidden, upstream, experts, lead):
    groups, owners = plan_now.shape
    planes = owners // 2
    plan_now, plan_next, hidden, upstream = [
        pltpu.with_memory_space_constraint(array, pltpu.HBM)
        for array in (plan_now, plan_next, hidden, upstream)
    ]
    tokens, inner = hidden.shape
    width = upstream.shape[1]
    cols = width // groups
    rows = inner // owners
    parts = 4 if tokens % 512 == 0 else 1
    hbm = pl.BlockSpec(memory_space=pltpu.HBM)
    vmem = pl.BlockSpec(memory_space=pltpu.VMEM)

    def blocks(n):
        return jax.ShapeDtypeStruct((n, groups, rows, cols), jnp.bfloat16)

    turned, copied, keep, send, chosen = pl.pallas_call(
        first_kernel,
        in_specs=[pl.BlockSpec(memory_space=pltpu.SMEM)] + [hbm] * 4,
        out_specs=[vmem] * 5,
        out_shape=[
            jax.ShapeDtypeStruct((inner, tokens), jnp.bfloat16),
            jax.ShapeDtypeStruct((tokens, width), jnp.bfloat16),
            blocks(lead),
            blocks(lead),
            jax.ShapeDtypeStruct((2, 2 * groups, experts, cols), jnp.float32),
        ],
        scratch_shapes=[
            pltpu.VMEM((tokens, inner), jnp.bfloat16),
            pltpu.SMEM(plan_now.shape, jnp.int32),
            pltpu.SMEM(plan_next.shape, jnp.int32),
            pltpu.SemaphoreType.DMA((parts,)),
            pltpu.SemaphoreType.DMA((groups,)),
            pltpu.SemaphoreType.DMA((2,)),
        ],
        compiler_params=pltpu.CompilerParams(vmem_limit_bytes=24 * 2**20),
        cost_estimate=pl.CostEstimate(
            flops=4 * tokens * rows * lead * width,
            bytes_accessed=2 * (tokens * inner + tokens * width),
            transcendentals=0,
        ),
        name="first_blocks",
    )(counts, plan_now, plan_next, hidden, upstream)
    return turned, copied, keep, send, chosen


def rest_blocks(turned, upstream, groups, planes, rest):
    tokens, width = upstream.shape
    inner = turned.shape[0]
    cols = width // groups
    rows = inner // (2 * planes)
    vmem = pl.BlockSpec(memory_space=pltpu.VMEM)
    out = jax.ShapeDtypeStruct((rest, groups, rows, cols), jnp.bfloat16)
    return pl.pallas_call(
        rest_kernel,
        in_specs=[vmem, vmem],
        out_specs=[vmem, vmem],
        out_shape=[out, out],
        compiler_params=pltpu.CompilerParams(vmem_limit_bytes=24 * 2**20),
        cost_estimate=pl.CostEstimate(
            flops=4 * tokens * rows * rest * width,
            bytes_accessed=4 * rows * rest * width,
            transcendentals=0,
        ),
        name="rest_blocks",
    )(turned, upstream)


class Mail:
    def __init__(self, ties):
        self.ties = ties
        self.arrived = {}

    def send(self, name, value, pairs):
        self.arrived[name] = lax.ppermute(self.hold(name, value), AXES, pairs)

    def hold(self, name, value):
        after = [self.arrived[n] for n in self.ties.get(name, ()) if n in self.arrived]
        return lax.optimization_barrier((value, *after))[0] if after else value

    def __getitem__(self, name):
        return self.arrived[name]


def per_device_planes(
    hidden_acts, out_grads, row_counts, plan_now, plan_next, master, moment_one, moment_two
):
    groups = lax.axis_size("dp")
    owners = lax.axis_size("expert")
    planes = owners // 2
    group = lax.axis_index("dp")
    owner = lax.axis_index("expert")
    plane, core = owner >> 1, owner & 1
    experts, rows, cols = master.shape

    everyone = range(groups * owners)
    to_core = [(d, d ^ 1) for d in everyone]
    to_group = [[(d, d ^ (j * owners)) for d in everyone] for j in range(groups)]
    to_plane = [[(d, d ^ 2 * s) for d in everyone] for s in range(planes)]
    others = range(1, groups)
    lead = 3

    turned, upstream, first_keep, first_send, chosen = first_blocks(
        row_counts, plan_now, plan_next, hidden_acts[0, 0], out_grads[0, 0], experts, lead
    )
    now, later = chosen[0], chosen[1]

    mail = Mail(SUM_TIES)
    mail.send("first", first_send, to_core)
    keep, held = [[blocks[n] for n in range(lead)] for blocks in (first_keep, mail["first"])]

    def plane_sum(n):
        total = jnp.zeros((experts, rows, cols), jnp.float32)
        for j in range(groups):
            block = mail[n, j] if j else jnp.stack([keep[n][0], held[n][0]])
            for i in range(2):
                total = total + now[2 * j + i][:, None] * block[i].astype(jnp.float32)
        return total

    for n in range(planes):
        if n == lead:
            rest_keep, rest_send = rest_blocks(
                mail.hold("rest", turned), upstream, groups, planes, planes - lead
            )
            for m in range(planes - lead):
                mail.send(("other", m), rest_send[m], to_core)
                keep.append(rest_keep[m])
                held.append(mail["other", m])
        for j in others:
            mail.send((n, j), jnp.stack([keep[n][j], held[n][j]]), to_group[j])
        if n:
            total = plane_sum(n - 1)
            if n == 2:
                total = total + mail["sum", 0].astype(jnp.float32)
            mail.send(("sum", n - 1), total.astype(jnp.bfloat16), to_plane[3 if n == 2 else 1])
    grad_sum = plane_sum(planes - 1)
    for n in range(1, planes - 1):
        grad_sum = grad_sum + mail["sum", n].astype(jnp.float32)

    master_new, moment_one_new, moment_two_new = adam(grad_sum, master, moment_one, moment_two)
    rounded = master_new.astype(jnp.bfloat16)

    def chosen_blocks(shard):
        shard = shard.astype(jnp.float32)
        return [
            jnp.stack(
                [jnp.sum(later[2 * j + i][:, None] * shard, axis=0).astype(jnp.bfloat16) for i in range(2)]
            )
            for j in range(groups)
        ]

    def in_order(blocks):
        for bit in range(groups.bit_length() - 1):
            swap = (group >> bit) & 1 == 1
            blocks = [jnp.where(swap, blocks[m ^ (1 << bit)], blocks[m]) for m in range(groups)]
        return jnp.concatenate(blocks, axis=-1)

    back = PLANE_ORDER[::-1]
    own = {}
    mail = Mail(SPREAD_TIES)

    def send_shard(n):
        mail.send(("shard", n), mail["shard", 2] if n == 3 else rounded, to_plane[3 if n == 2 else 1])

    def pass_on(n):
        blocks = jnp.stack([own[n][1]] + [mail[n, j][1] for j in others])
        mail.send(("core", n), blocks, to_core)

    send_shard(1)
    for n in range(planes):
        own[n], *blocks = chosen_blocks(mail.hold(("choose", n), mail["shard", n]) if n else rounded)
        for j, block in enumerate(blocks, 1):
            mail.send((n, j), block, to_group[j])
        if n == 0:
            for m in range(2, planes):
                send_shard(m)
        else:
            pass_on(n - 1)
    pass_on(planes - 1)

    replica = jnp.zeros((planes, 2, rows, groups * cols), jnp.bfloat16)
    for n, s in enumerate(back):
        mine = in_order([own[n][0]] + [mail[n, j][0] for j in others])
        other = in_order([mail["core", n][j] for j in range(groups)])
        both = jnp.stack([jnp.where(core == 0, mine, other), jnp.where(core == 0, other, mine)])
        replica = lax.dynamic_update_index_in_dim(replica, both, plane ^ s, 0)
    replica = replica.reshape(2 * planes * rows, groups * cols)
    return (master_new, moment_one_new, moment_two_new, replica[None, None])


def per_device_whole(
    hidden_acts, out_grads, row_counts, plan_now, plan_next, master, moment_one, moment_two
):
    ex_count = lax.axis_size("expert")
    dp_index = lax.axis_index("dp")
    experts = master.shape[0]
    piece_rows = master.shape[1]
    hidden = hidden_acts[0, 0]
    upstream = out_grads[0, 0]
    width = upstream.shape[1]
    row_index = jnp.arange(hidden.shape[0], dtype=jnp.int32)
    row_mask = (row_index < row_counts[0, 0]).astype(hidden.dtype)[:, None]
    partial_value = lax.dot_general(
        hidden * row_mask, upstream, (((0,), (0,)), ((), ())), preferred_element_type=jnp.float32
    ).astype(jnp.bfloat16)
    expert_ids = jnp.arange(experts, dtype=jnp.int32)
    pieces = lax.all_to_all(
        partial_value.reshape(ex_count, piece_rows, width),
        "expert",
        split_axis=0,
        concat_axis=0,
        tiled=True,
    )
    sender_ids = lax.dynamic_index_in_dim(plan_now, dp_index, 0, keepdims=False)
    onehot = (sender_ids[None, :] == expert_ids[:, None]).astype(jnp.bfloat16)
    totals = jnp.einsum("es,srd->erd", onehot, pieces, preferred_element_type=jnp.float32)
    grad_sum = lax.psum_scatter(
        totals.astype(jnp.bfloat16), "dp", scatter_dimension=2, tiled=True
    ).astype(jnp.float32)
    master_new, moment_one_new, moment_two_new = adam(grad_sum, master, moment_one, moment_two)
    rounded = master_new.astype(jnp.bfloat16)
    full_cols = lax.all_gather(rounded, "dp", axis=2, tiled=True)
    targets = lax.dynamic_index_in_dim(plan_next, dp_index, 0, keepdims=False)
    outgoing = jnp.take(full_cols, targets, axis=0)
    incoming = lax.all_to_all(outgoing, "expert", split_axis=0, concat_axis=0, tiled=True)
    replica = incoming.reshape(ex_count * piece_rows, width)
    return (master_new, moment_one_new, moment_two_new, replica[None, None])


def per_device(hidden_acts, out_grads, row_counts, plan_now, plan_next, master, *moments):
    groups = lax.axis_size("dp")
    owners = lax.axis_size("expert")
    experts, rows, cols = master.shape
    few = experts <= 2 * groups and owners == 2 * len(PLANE_ORDER)
    even = groups & (groups - 1) == 0 and rows % 16 == 0 and cols % 128 == 0
    body = per_device_planes if few and even else per_device_whole
    return body(hidden_acts, out_grads, row_counts, plan_now, plan_next, master, *moments)


def solution(mesh):
    return jax.shard_map(
        per_device,
        mesh=mesh,
        in_specs=(
            P("dp", "expert", None, None),
            P("dp", "expert", None, None),
            P("dp", "expert"),
            P(),
            P(),
            P(None, "expert", "dp"),
            P(None, "expert", "dp"),
            P(None, "expert", "dp"),
        ),
        out_specs=(
            P(None, "expert", "dp"),
            P(None, "expert", "dp"),
            P(None, "expert", "dp"),
            P("dp", "expert", None, None),
        ),
        check_vma=False,
    )
```
